512 devices in a mesh: side: 2 (over core), group: 64 (over y, z), tensor: 4 (over x).
Axes of the slice: x: 4, y: 4, z: 16, core: 2. Of those that a mesh axis runs over, the one named last changes fastest.
Arguments:
- tokens: bfloat16 [2, 2048, 4096], P(None, 'group', ('side', 'tensor'))
- norm_gain: bfloat16 [4096], P(('side', 'tensor')), may hold values from 0.099609375 to 1.8984375
- router_weight: bfloat16 [4096, 64], P(('side', 'tensor')), may hold values from -0.09375 to 0.09375
- expert_ids: int32 [2, 2048, 4], P(None, 'group'), may hold values from 0 to 63, all different within a row; in each aligned block of 32 rows (0 to 31, 32 to 63, ..., all dimensions but the last counted through in order) at most 4 rows name the same one
- w_gate: bfloat16 [64, 4096, 1024], P('group', None, ('side', 'tensor')), may hold values from -0.09375 to 0.09375
- w_up: bfloat16 [64, 4096, 1024], P('group', None, ('side', 'tensor')), may hold values from -0.09375 to 0.09375
- w_down: bfloat16 [64, 1024, 4096], P('group', None, ('side', 'tensor')), may hold values from -0.1875 to 0.1875
Outputs:
- mixed: bfloat16 [2, 2048, 4096], P(None, 'group', ('side', 'tensor'))
The draws below stay inside these ranges and needn't reach their ends.
Inputs may be any that keep to these rules, and one draw needn't show every extreme that they name: `expert_ids`: each row names 4 different experts. Within each aligned block of 32 rows of a micro-batch no expert is named by more than 4 rows, a bound that some block reaches in every draw.
All inputs are finite; a program needn't handle non-finite values.
Results may differ from the reference program's by a relative error of at most 0.0041.
Values may be sent and summed in bfloat16 or wider, within the bound.
A program may use at most 64 MiB of HBM per device.

```python
import math
import jax
import jax.numpy as jnp
import numpy as np
from jax import lax

D = 4096
FH = 1024
TOP = 4
MB = 2
ROW_DEV = 32
EXPERTS = 64
ROWS = 2048
SLOT = 4
N_GROUP = 64


def draw_tokens(key, part):
    key = jax.random.fold_in(key, 11)
    key_rows, key_cols, key_base = jax.random.split(key, 3)
    row_scale = jnp.exp(jax.random.uniform(key_rows, (MB, ROWS, 1), jnp.float32) * math.log(10.0))
    ramp = 1.0 + 2.0 * jnp.arange(D, dtype=jnp.float32) / (D - 1)
    col_scale = jnp.exp(jax.random.uniform(key_cols, (1, 1, D), jnp.float32) * math.log(10.0 / 3.0)) * ramp
    base = jnp.clip(jax.random.normal(key_base, (MB, ROWS, D), jnp.float32), -6.0, 6.0)
    values = 0.1 * base * row_scale * col_scale
    return values.astype(jnp.bfloat16)


def level_of(key, shape, cuts, smallest, largest):
    def one(dim, parts):
        steps = jax.random.uniform(jax.random.fold_in(jax.random.fold_in(key, 6), dim), (parts,), jnp.float32, smallest / len(cuts), largest / len(cuts))
        return jnp.repeat(jnp.exp(steps), shape[dim] // parts).reshape((-1,) + (1,) * (len(shape) - dim - 1))

    level = one(*cuts[0])
    for cut in cuts[1:]:
        level = level * one(*cut)
    return level


def deal_out(stream_key, own, number, rows, amount, top, limit, slope):
    sequence = jax.random.permutation(stream_key, amount)
    crowded, usual = portions_of(amount, rows * top, limit, slope, True), portions_of(amount, rows * top, limit, slope, False)
    places = jnp.arange(amount)

    def named(sizes, rotation):
        used = int((sizes > 0).sum())
        fixed = max(1, used // 4)
        shifted = fixed + (places - fixed + rotation * (used - fixed)) % max(1, amount - fixed)
        return jnp.zeros((amount,), jnp.int32).at[sequence[jnp.where(places < fixed, places, shifted)]].set(jnp.asarray(sizes, jnp.int32))

    sizes = jnp.where(number % 4 == 0, named(crowded, number // 4), named(usual, number - number // 4 - 1))
    mixed = jax.random.permutation(jax.random.fold_in(own, 3), amount)
    source_of, receiver = mixed[0:amount // 2 * 2:2], mixed[1:amount // 2 * 2:2]
    margin = jnp.minimum(sizes[source_of] - 1, limit - sizes[receiver]) // 2
    margin = jnp.where((source_of == sequence[0]) | (receiver == sequence[0]) | (sizes[receiver] == 0), 0, jnp.maximum(margin, 0))
    shifted = jax.random.randint(jax.random.fold_in(own, 4), (amount // 2,), 0, 1 << 20) % (margin + 1)
    sizes = sizes.at[source_of].add(-shifted).at[receiver].add(shifted)
    members = jnp.searchsorted(jnp.cumsum(sizes), jnp.arange(rows * top), side="right").astype(jnp.int32)
    table = members.reshape(top, rows).T
    table = table[jax.random.permutation(jax.random.fold_in(own, 1), rows)]
    rotation = jax.random.randint(jax.random.fold_in(own, 2), (rows, 1), 0, top)
    return jnp.take_along_axis(table, (jnp.arange(top)[None, :] + rotation) % top, axis=1)


def portions_of(amount, total, bound, lean, full):
    weights = [(1 << 20) // math.isqrt(rank ** lean) + 1 for rank in range(1, amount + 1)]
    largest = bound if full else min(bound, max(-(-total // amount), total * weights[0] // sum(weights)))
    least = 1 if total - largest >= amount - 1 else 0
    counts, rest = [largest] + [least] * (amount - 1), total - largest - least * (amount - 1)
    while rest > 0:
        candidates = [i for i in range(1, amount) if counts[i] < largest] or [i for i in range(1, amount) if counts[i] < bound]
        whole, remaining = sum([weights[i] for i in candidates]), rest
        for i in candidates:
            addition = min(bound - counts[i], max(1, remaining * weights[i] // whole), rest)
            counts[i] = counts[i] + addition
            rest = rest - addition
    return np.array(counts)


def scatter_about(own_key, dims, width, reach, pieces=(), kind=jnp.bfloat16):
    array = width * jax.random.normal(own_key, dims, jnp.float32)
    if pieces:
        array = array * level_of(own_key, dims, pieces, -0.22, 0.18)
    return jnp.clip(array, -reach, reach).astype(kind)


def setup_inputs(seed: int = 0) -> dict:
    keys = jax.random.split(jax.random.key(seed), 8)
    tokens = draw_tokens(jax.random.fold_in(keys[7], 71), 0)
    norm_gain = jnp.clip(1.0 + 0.18 * jax.random.normal(keys[1], (D,), jnp.float32), 0.099609375, 1.8984375).astype(jnp.bfloat16)
    router_weight = scatter_about(keys[2], (D, EXPERTS), D ** -0.5, 0.09375, ((0, 8),))
    expert_ids_keys = jax.random.split(jax.random.fold_in(keys[3], 1), MB * ROWS // ROW_DEV)
    expert_ids_turns = jax.random.permutation(jax.random.fold_in(keys[3], 3), MB * ROWS // ROW_DEV)
    expert_ids = jax.vmap(lambda own, number: deal_out(jax.random.fold_in(keys[3], 2), own, number, ROW_DEV, EXPERTS, TOP, SLOT, 2))(expert_ids_keys, expert_ids_turns).reshape((MB, ROWS, TOP))
    w_gate = scatter_about(keys[4], (EXPERTS, D, FH), D ** -0.5, 0.09375, ((0, 64), (2, 8)))
    w_up = scatter_about(keys[5], (EXPERTS, D, FH), D ** -0.5, 0.09375, ((0, 64), (2, 8)))
    w_down = scatter_about(keys[6], (EXPERTS, FH, D), FH ** -0.5, 0.1875, ((0, 64), (2, 8)))
    return {"tokens": tokens, "norm_gain": norm_gain, "router_weight": router_weight, "expert_ids": expert_ids, "w_gate": w_gate, "w_up": w_up, "w_down": w_down}


def expert_apply(operands):
    buffer, gate_w, up_w, down_w = operands
    gate_part = jnp.dot(buffer, gate_w, preferred_element_type=jnp.float32)
    up_part = jnp.dot(buffer, up_w, preferred_element_type=jnp.float32)
    hidden = (jax.nn.silu(gate_part) * up_part).astype(jnp.bfloat16)
    return jnp.dot(hidden, down_w, preferred_element_type=jnp.float32).astype(jnp.bfloat16)

def reference(tokens, norm_gain, router_weight, expert_ids, w_gate, w_up, w_down):
    values = tokens.astype(jnp.float32)
    inv_rms = lax.rsqrt(lax.optimization_barrier(jnp.mean(values * values, axis=-1, keepdims=True)) + 1e-06)
    scaled = values * norm_gain.astype(jnp.float32)
    normed = (scaled * inv_rms).astype(jnp.bfloat16)
    logits = inv_rms * jnp.einsum('mrd,de->mre', scaled, router_weight.astype(jnp.float32), precision=lax.Precision.HIGHEST)
    scores = jax.nn.sigmoid(logits)
    chosen = (expert_ids[..., None] == jnp.arange(EXPERTS, dtype=jnp.int32)).astype(jnp.float32)
    picked = lax.optimization_barrier(jnp.sum(chosen * scores[:, :, None, :], axis=-1))
    gates = 2.5 * picked / lax.optimization_barrier(jnp.sum(picked, axis=-1, keepdims=True))
    flat_choice = chosen.reshape(MB, N_GROUP, ROW_DEV * TOP, EXPERTS)
    earlier = jnp.cumsum(flat_choice, axis=2) - flat_choice
    position = lax.optimization_barrier(jnp.sum(earlier * flat_choice, axis=-1)).astype(jnp.int32).reshape(MB, ROWS, TOP)
    owner_block = (jnp.arange(ROWS, dtype=jnp.int32) // ROW_DEV).astype(jnp.int32)
    target = owner_block[None, :, None] * SLOT + position
    results = []
    for which in range(MB):
        spread_rows = jnp.broadcast_to(normed[which][:, None, :], (ROWS, TOP, D))
        buffer = jnp.zeros((EXPERTS, N_GROUP * SLOT, D), jnp.bfloat16)
        buffer = buffer.at[expert_ids[which], target[which]].set(spread_rows)
        outputs = lax.map(expert_apply, (buffer, w_gate, w_up, w_down))
        gathered = outputs[expert_ids[which], target[which]].astype(jnp.float32)
        combined = jnp.einsum('rk,rkd->rd', gates[which], gathered, precision=lax.Precision.HIGHEST)
        results.append((values[which] + combined).astype(jnp.bfloat16))
    return jnp.stack(results)
```

```python
import jax
import jax.numpy as jnp
from jax import lax
from jax.experimental import pallas as pl
from jax.experimental.pallas import tpu as pltpu
from jax.sharding import PartitionSpec as P

MESH = pl.DeviceIdType.MESH
BF = jnp.bfloat16
F32 = jnp.float32
YN, ZN = 4, 16
XN, CN = 4, 2
SLOT = 4
LANES = 128
HALVES = 2


def iota(shape, dim):
    return lax.broadcasted_iota(jnp.int32, shape, dim)


def remote(src, dst, send, recv, peer):
    return pltpu.make_async_remote_copy(
        src_ref=src,
        dst_ref=dst,
        send_sem=send,
        recv_sem=recv,
        device_id=peer,
        device_id_type=MESH,
    )


def kernel(
    tok, gain, router, ids, wg, wu, wd, out,
    wgu, wdv, sel, gates, gx, sb, rb, xb, mt, hb, ob, back,
    wsem, gx_s, gx_r, z_s, z_r, x_s, x_r, m_s, m_r, h_s, h_r, o_s, o_r,
):
    batches, rows, chan = tok.shape
    groups = YN * ZN
    blocks = chan // LANES
    per = blocks * SLOT
    hid = wg.shape[2]
    depth = CN * XN * chan
    span = groups // HALVES
    slots = span * SLOT
    stages = [(m, h * span) for m in range(batches) for h in range(HALVES)]

    g, t, c = (lax.axis_index(a) for a in ("group", "tensor", "side"))
    y, z = lax.div(g, ZN), lax.rem(g, ZN)

    def ahead(d):
        return {"group": lax.rem(y + lax.div(d, ZN), YN) * ZN + lax.rem(z + lax.rem(d, ZN), ZN)}

    def behind(d):
        return {
            "group": lax.rem(y + YN - lax.div(d, ZN), YN) * ZN
            + lax.rem(z + ZN - lax.rem(d, ZN), ZN)
        }

    def near(cs, xr):
        return {"side": lax.rem(c + cs, CN), "tensor": lax.rem(t + xr, XN)}

    right, left, other = near(0, 1), near(0, XN - 1), near(1, 0)
    mates = [(cs, xr) for cs in range(CN) for xr in range(XN) if cs + xr]

    barrier = pltpu.get_barrier_semaphore()

    def greet(i, carry):
        pl.semaphore_signal(barrier, inc=1, device_id=ahead(i + 1), device_id_type=MESH)
        return carry

    lax.fori_loop(0, groups - 1, greet, 0)
    for cs, xr in mates:
        pl.semaphore_signal(barrier, inc=1, device_id=near(cs, xr), device_id_type=MESH)

    for cs in range(CN):
        for xr in range(XN):
            rel = cs * XN + xr
            home = lax.rem(c + cs, CN) * XN + lax.rem(t + xr, XN)
            deep = pl.ds(pl.multiple_of(home * chan, chan), chan)
            pltpu.make_async_copy(wg.at[0, deep, :], wgu.at[rel, :, pl.ds(0, hid)], wsem.at[0]).start()
            pltpu.make_async_copy(wu.at[0, deep, :], wgu.at[rel, :, pl.ds(hid, hid)], wsem.at[0]).start()
            thin = pl.ds(pl.multiple_of(home * hid, hid), hid)
            pltpu.make_async_copy(wd.at[0, thin, :], wdv.at[rel], wsem.at[1]).start()

    tall = blocks * rows
    lane, sub = iota((tall, LANES), 1), iota((tall, LANES), 0)
    earlier = (((sub // rows) == (lane // rows)) & (lane < sub)).astype(BF)
    wide = groups * per
    spread = (iota((LANES, wide), 1) // per == iota((LANES, wide), 0)).astype(BF)
    column, line = iota((tall, wide), 1), iota((tall, wide), 0)
    fits = ((column // SLOT) % blocks) == (line // rows)
    which_slot = (column % SLOT).astype(F32)

    def stacked(m):
        return jnp.concatenate([tok[m, :, b * LANES : (b + 1) * LANES] for b in range(blocks)], axis=0)

    def relative(m):
        named = ids[m]
        rel = (((named // ZN) - y + YN) % YN) * ZN + (((named % ZN) - z + ZN) % ZN)
        return jnp.concatenate([rel] * blocks, axis=0)

    def choose(m):
        rel = relative(m)
        picks = rel.shape[1]
        hit = sum((rel[:, k : k + 1] == lane).astype(F32) for k in range(picks))
        position = jnp.dot(earlier, hit.astype(BF), preferred_element_type=F32)
        code = jnp.where(hit > 0, position, -1.0).astype(BF)
        full = jnp.dot(code, spread, preferred_element_type=F32)
        chosen = jnp.where(fits & (full == which_slot), 1.0, 0.0).astype(BF)
        sel[m] = chosen
        moved = lax.dot_general(
            chosen, stacked(m), (((0,), (0,)), ((), ())), preferred_element_type=F32
        )
        sb[m] = moved.astype(BF).reshape(groups, per, LANES)
        rb[m, 0] = sb[m, 0]

    for m in range(batches):
        choose(m)

    gain_row = gain[...].astype(F32)
    values = tok[...].reshape(batches * rows, chan).astype(F32)
    scaled = values * gain_row
    high = scaled.astype(BF)
    low = (scaled - high.astype(F32)).astype(BF)
    part = jnp.dot(high, router[...], preferred_element_type=F32)
    part = part + jnp.dot(low, router[...], preferred_element_type=F32)
    experts = router.shape[1]
    gx[0, :, 0:experts] = part
    gx[0, :, experts:LANES] = jnp.broadcast_to(
        jnp.sum(values * values, axis=1, keepdims=True), (batches * rows, LANES - experts)
    )

    pl.semaphore_wait(barrier, groups - 1 + len(mates))

    def order(i, lo):
        k, dy = lax.div(i, span // ZN), span // ZN - 1 - lax.rem(i, span // ZN)
        half = lax.div(k + 1, 2)
        dz = lax.rem(ZN // 2 + half - 2 * half * lax.rem(k, 2), ZN)
        return lo + dy * ZN + dz

    def z_out(s):
        m, lo = stages[s]

        def one(i, carry):
            d = order(i, lo)
            remote(sb.at[m, d], rb.at[m, d], z_s.at[s], z_r.at[s], ahead(d)).start()
            return carry

        lax.fori_loop(0, span - (lo == 0), one, 0)

    def z_all(s, src, dst, send, recv):
        m, lo = stages[s]
        first = max(lo, 1)
        some = pl.ds(first, lo + span - first)
        return remote(src.at[m, some], dst.at[m, some], send.at[s], recv.at[s], right)

    def gx_send():
        for cs, xr in mates:
            there = cs * XN + (XN - xr) % XN
            remote(gx.at[0], gx.at[there], gx_s, gx_r, near(cs, xr)).start()

    tile = ZN * per
    i_to, i_from = iota((tile, tile), 0), iota((tile, tile), 1)
    to_b, to_d, to_p = i_to // (ZN * SLOT), (i_to // SLOT) % ZN, i_to % SLOT
    apart = (i_from == to_d * per + to_b * SLOT + to_p).astype(BF)
    from_b, from_d, from_p = i_from // (ZN * SLOT), (i_from // SLOT) % ZN, i_from % SLOT
    together = (i_to == from_d * per + from_b * SLOT + from_p).astype(BF)
    chunk = ZN * SLOT
    diagonal = iota((slots, slots), 0) == iota((slots, slots), 1)

    started = {}

    def x_copy(s, i, src, dst, peer):
        q = remote(src, dst, x_s.at[s, i], x_r.at[s, i], peer)
        q.start()
        started[s, i] = q

    half_rows = slots // 2
    lower, upper = pl.ds(0, half_rows), pl.ds(half_rows, half_rows)

    def arrive(s):
        m, lo = stages[s]
        z_all(s, sb, rb, z_s, z_r).wait_recv()
        squares = []
        for n in range(span // ZN):
            raw = rb[m, lo + n * ZN : lo + (n + 1) * ZN].reshape(tile, LANES)
            moved = jnp.dot(apart, raw, preferred_element_type=F32)
            part = jnp.concatenate([moved[b * chunk : (b + 1) * chunk] for b in range(blocks)], axis=1)
            squares.append(jnp.sum(part * part, axis=1, keepdims=True))
            xb[s, 0, 0, n * chunk : (n + 1) * chunk, :] = (part * gain_row).astype(BF)
        own = xb.at[s, 0, 0]
        x_copy(s, 0, own.at[lower], xb.at[s, 0, XN - 1, lower], right)
        x_copy(s, 1, own.at[upper], xb.at[s, 0, 1, upper], left)
        x_copy(s, 2, own.at[upper], xb.at[s, 0, XN - 1, upper], right)
        x_copy(s, 3, own.at[lower], xb.at[s, 0, 1, lower], left)
        x_copy(s, 4, own, xb.at[s, 1, 0], other)
        square = jnp.concatenate(squares, axis=0)
        flat = jnp.sum(jnp.where(diagonal, square, 0.0), axis=0, keepdims=True)
        mt[s, 0] = jnp.broadcast_to(flat, mt.shape[2:])
        for cs, xr in mates:
            there = cs * XN + (XN - xr) % XN
            remote(mt.at[s, 0], mt.at[s, there], m_s.at[s], m_r.at[s], near(cs, xr)).start()

    def relay(s):
        started[s, 0].wait_recv()
        x_copy(s, 5, xb.at[s, 0, XN - 1, lower], xb.at[s, 0, 2, lower], right)
        started[s, 1].wait_recv()
        x_copy(s, 6, xb.at[s, 0, 1, upper], xb.at[s, 0, 2, upper], left)
        started[s, 2].wait_recv()
        x_copy(s, 7, xb.at[s, 0, XN - 1], xb.at[s, 1, XN - 1], other)
        started[s, 3].wait_recv()
        x_copy(s, 8, xb.at[s, 0, 1], xb.at[s, 1, 1], other)

    def hidden(s):
        started[s, 5].wait_recv()
        started[s, 6].wait_recv()
        x_copy(s, 9, xb.at[s, 0, 2], xb.at[s, 1, 2], other)
        rest = pl.ds(1, CN * XN - 1)
        remote(mt.at[s, rest], mt.at[s, rest], m_s.at[s], m_r.at[s], other).wait_recv()
        total = sum(mt[s, r] for r in range(CN * XN))
        inv = lax.rsqrt(total[0:1] / depth + 1e-06)
        inv = jnp.sum(jnp.where(diagonal, inv, 0.0), axis=1, keepdims=True)
        both = jnp.zeros((slots, 2 * hid), F32)
        for xr in range(XN):
            both = both + jnp.dot(xb[s, 0, xr], wgu[xr], preferred_element_type=F32)
        for i, xr in ((4, 0), (7, XN - 1), (8, 1), (9, 2)):
            started[s, i].wait_recv()
            both = both + jnp.dot(xb[s, 1, xr], wgu[XN + xr], preferred_element_type=F32)
        both = both * inv
        gate, up = both[:, :hid], both[:, hid:]
        hb[s, 0, 0] = (gate / (1.0 + jnp.exp(-gate)) * up).astype(BF)
        for xr in (2, 1, 3):
            q = remote(hb.at[s, 0, 0], hb.at[s, 0, XN - xr], h_s.at[s, xr], h_r.at[s, XN - xr], near(0, xr))
            q.start()
            started[s, "h", xr] = q
        q = remote(hb.at[s, 0, 0], hb.at[s, 1, 0], h_s.at[s, 0], h_r.at[s, 0], other)
        q.start()
        started[s, "h", 0] = q

    def hidden_relay(s):
        for xr in (1, 3, 2):
            remote(hb.at[s, 0, xr], hb.at[s, 0, xr], h_s.at[s, xr], h_r.at[s, xr], other).wait_recv()
            q = remote(hb.at[s, 0, xr], hb.at[s, 1, xr], h_s.at[s, XN + xr], h_r.at[s, XN + xr], other)
            q.start()
            started[s, "h", XN + xr] = q

    def give_back(s):
        m, lo = stages[s]
        done = jnp.zeros((slots, chan), F32)
        for xr in range(XN):
            done = done + jnp.dot(hb[s, 0, xr], wdv[xr], preferred_element_type=F32)
        for xr in (0, 1, 3, 2):
            started[s, "h", XN + xr if xr else 0].wait_recv()
            done = done + jnp.dot(hb[s, 1, xr], wdv[XN + xr], preferred_element_type=F32)
        done = done.astype(BF)
        for n in range(span // ZN):
            part = done[n * chunk : (n + 1) * chunk]
            part = jnp.concatenate([part[:, b * LANES : (b + 1) * LANES] for b in range(blocks)], axis=0)
            moved = jnp.dot(together, part, preferred_element_type=F32).astype(BF)
            ob[m, lo + n * ZN : lo + (n + 1) * ZN] = moved.reshape(ZN, per, LANES)

        def one(i, carry):
            d = order(i, lo)
            remote(ob.at[m, d], back.at[m, d], o_s.at[s], o_r.at[s], behind(d)).start()
            return carry

        lax.fori_loop(0, span - (lo == 0), one, 0)
        if lo == 0:
            back[m, 0] = ob[m, 0]

    def weigh():
        rest = pl.ds(1, CN * XN - 1)
        remote(gx.at[rest], gx.at[rest], gx_s, gx_r, other).wait_recv()
        for m in range(batches):
            total = sum(gx[r, m * rows : (m + 1) * rows] for r in range(CN * XN))
            place = iota((rows, LANES), 1)
            squares = jnp.sum(jnp.where(place == experts, total, 0.0), axis=1, keepdims=True)
            inv = lax.rsqrt(squares / depth + 1e-06)
            scores = 1.0 / (1.0 + jnp.exp(-(inv * total)))
            named = ids[m]
            picked = [
                jnp.sum(jnp.where(named[:, k : k + 1] == place, scores, 0.0), axis=1, keepdims=True)
                for k in range(named.shape[1])
            ]
            whole = sum(picked)
            rel = relative(m)
            weight = jnp.zeros((tall, LANES), F32)
            for k, one in enumerate(picked):
                share = jnp.concatenate([2.5 * one / whole] * blocks, axis=0)
                weight = weight + jnp.where(rel[:, k : k + 1] == lane, share, 0.0)
            high = weight.astype(BF)
            low = (weight - high.astype(F32)).astype(BF)
            for i, some in enumerate((high, low)):
                full = jnp.dot(some, spread, preferred_element_type=F32)
                gates[i, m] = full.astype(BF) * sel[m]

    def combine(m):
        total = stacked(m).astype(F32)
        for s, (which, lo) in enumerate(stages):
            if which == m:
                z_all(s, ob, back, o_s, o_r).wait_recv()
                part = back[m, lo : lo + span].reshape(span * per, LANES)
                for i in range(2):
                    total = total + jnp.dot(
                        gates[i, m, :, lo * per : (lo + span) * per], part, preferred_element_type=F32
                    )
        total = total.astype(out.dtype)
        for b in range(blocks):
            out[m, :, b * LANES : (b + 1) * LANES] = total[b * rows : (b + 1) * rows]

    def weights_ready():
        pltpu.make_async_copy(wgu, wgu, wsem.at[0]).wait()
        pltpu.make_async_copy(wdv, wdv, wsem.at[1]).wait()

    z_out(0)
    z_out(1)
    gx_send()
    z_out(2)
    weights_ready()
    arrive(0)
    z_out(3)
    weigh()
    relay(0)
    arrive(1)
    hidden(0)
    relay(1)
    arrive(2)
    hidden_relay(0)
    hidden(1)
    relay(2)
    give_back(0)
    arrive(3)
    hidden_relay(1)
    hidden(2)
    relay(3)
    give_back(1)
    hidden_relay(2)
    hidden(3)
    give_back(2)
    hidden_relay(3)
    give_back(3)
    for m in range(batches):
        combine(m)

    for q in started.values():
        q.wait_send()
    for s in range(len(stages)):
        z_all(s, sb, rb, z_s, z_r).wait_send()
        z_all(s, ob, back, o_s, o_r).wait_send()
        rest = pl.ds(1, CN * XN - 1)
        remote(mt.at[s, rest], mt.at[s, rest], m_s.at[s], m_r.at[s], other).wait_send()
    rest = pl.ds(1, CN * XN - 1)
    remote(gx.at[rest], gx.at[rest], gx_s, gx_r, other).wait_send()


def per_device(tokens, norm_gain, router_weight, expert_ids, w_gate, w_up, w_down):
    batches, rows, chan = tokens.shape
    groups = YN * ZN
    per = chan // LANES * SLOT
    hid = w_gate.shape[2]
    stages = batches * HALVES
    slots = groups // HALVES * SLOT
    mates = CN * XN
    tall = chan // LANES * rows
    vmem = pl.BlockSpec(memory_space=pltpu.VMEM)
    hbm = pl.BlockSpec(memory_space=pl.ANY)
    dma = pltpu.SemaphoreType.DMA
    blocks = pltpu.VMEM((batches, groups, per, LANES), BF)
    return pl.pallas_call(
        kernel,
        out_shape=jax.ShapeDtypeStruct(tokens.shape, tokens.dtype),
        in_specs=[vmem] * 4 + [hbm] * 3,
        out_specs=vmem,
        scratch_shapes=[
            pltpu.VMEM((mates, chan, 2 * hid), BF),
            pltpu.VMEM((mates, hid, chan), BF),
            pltpu.VMEM((batches, tall, groups * per), BF),
            pltpu.VMEM((2, batches, tall, groups * per), BF),
            pltpu.VMEM((mates, batches * rows, LANES), F32),
            blocks,
            blocks,
            pltpu.VMEM((stages, CN, XN, slots, chan), BF),
            pltpu.VMEM((stages, mates, 8, slots), F32),
            pltpu.VMEM((stages, CN, XN, slots, hid), BF),
            blocks,
            blocks,
            dma((2,)),
            dma,
            dma,
            dma((stages,)),
            dma((stages,)),
            dma((stages, 10)),
            dma((stages, 10)),
            dma((stages,)),
            dma((stages,)),
            dma((stages, mates)),
            dma((stages, mates)),
            dma((stages,)),
            dma((stages,)),
        ],
        compiler_params=pltpu.CompilerParams(
            collective_id=0, has_side_effects=True, vmem_limit_bytes=48 << 20
        ),
        name="routed_experts",
    )(tokens, norm_gain.reshape(1, chan), router_weight, expert_ids, w_gate, w_up, w_down)


def solution(mesh):
    placed = (
        P(None, "group", ("side", "tensor")),
        P(("side", "tensor")),
        P(("side", "tensor"), None),
        P(None, "group", None),
        P("group", None, ("side", "tensor")),
        P("group", None, ("side", "tensor")),
        P("group", None, ("side", "tensor")),
    )
    return jax.shard_map(
        per_device,
        mesh=mesh,
        in_specs=placed,
        out_specs=P(None, "group", ("side", "tensor")),
        check_vma=False,
    )
```

```python
import jax
import jax.numpy as jnp
from jax import lax
from jax.experimental import pallas as pl
from jax.experimental.pallas import tpu as pltpu
from jax.sharding import PartitionSpec as P

MESH = pl.DeviceIdType.MESH
BF = jnp.bfloat16
F32 = jnp.float32
YN, ZN = 4, 16
XN, CN = 4, 2
SLOT = 4
LANES = 128


def iota(shape, dim):
    return lax.broadcasted_iota(jnp.int32, shape, dim)


def remote(src, dst, send, recv, peer):
    return pltpu.make_async_remote_copy(
        src_ref=src,
        dst_ref=dst,
        send_sem=send,
        recv_sem=recv,
        device_id=peer,
        device_id_type=MESH,
    )


def kernel(
    tok_in, gain, router_in, ids_in, wg, wu, wd, out,
    tok, router, ids, wgu, wdv, sel, gates, gx, sb, rb, xb, mt, hb, ob, back,
    wsem, gx_s, gx_r, z_s, z_r, x_s, x_r, m_s, m_r, h_s, h_r, o_s, o_r,
):
    batches, rows, chan = tok.shape
    groups = YN * ZN
    blocks = chan // LANES
    per = blocks * SLOT
    hid = wg.shape[2]
    depth = CN * XN * chan
    slots = ZN * batches * SLOT
    step = ZN // batches

    g, t, c = (lax.axis_index(a) for a in ("group", "tensor", "side"))
    y, z = lax.div(g, ZN), lax.rem(g, ZN)

    y_at = [lax.rem(y + i, YN) * ZN for i in range(YN)]
    z_at = [lax.rem(z + i, ZN) for i in range(ZN)]

    def ahead(d):
        return {"group": y_at[d // ZN] + z_at[d % ZN]}

    def behind(d):
        return {"group": y_at[-(d // ZN) % YN] + z_at[-(d % ZN) % ZN]}

    def near(cs, xr):
        return {"side": lax.rem(c + cs, CN), "tensor": lax.rem(t + xr, XN)}

    right, left, other = near(0, 1), near(0, XN - 1), near(1, 0)
    mates = [(cs, xr) for cs in range(CN) for xr in range(XN) if cs + xr]

    sent, coming = [], {}

    def launch(key, q):
        q.start()
        sent.append(q)
        coming[key] = q

    def receive(*key):
        coming.pop(key).wait_recv()

    barrier = pltpu.get_barrier_semaphore()

    for d in sorted(range(1, groups), key=lambda d: -min(d % ZN, ZN - d % ZN)):
        pl.semaphore_signal(barrier, inc=1, device_id=ahead(d), device_id_type=MESH)
    for cs, xr in mates:
        pl.semaphore_signal(barrier, inc=1, device_id=near(cs, xr), device_id_type=MESH)

    copies = [
        pltpu.make_async_copy(src, dst, wsem.at[2 + i])
        for i, (src, dst) in enumerate(((ids_in, ids), (tok_in, tok), (router_in, router)))
    ]
    for q in copies:
        q.start()

    for cs in range(CN):
        for xr in range(XN):
            rel = cs * XN + xr
            home = lax.rem(c + cs, CN) * XN + lax.rem(t + xr, XN)
            deep = pl.ds(pl.multiple_of(home * chan, chan), chan)
            pltpu.make_async_copy(wg.at[0, deep, :], wgu.at[rel, :, pl.ds(0, hid)], wsem.at[0]).start()
            pltpu.make_async_copy(wu.at[0, deep, :], wgu.at[rel, :, pl.ds(hid, hid)], wsem.at[0]).start()
            thin = pl.ds(pl.multiple_of(home * hid, hid), hid)
            pltpu.make_async_copy(wd.at[0, thin, :], wdv.at[rel], wsem.at[1]).start()

    tall = blocks * rows
    lane, sub = iota((tall, LANES), 1), iota((tall, LANES), 0)
    earlier = (((sub // rows) == (lane // rows)) & (lane < sub)).astype(BF)
    wide = groups * per
    spread = (iota((LANES, wide), 1) // per == iota((LANES, wide), 0)).astype(BF)
    column, line = iota((tall, wide), 1), iota((tall, wide), 0)
    fits = ((column // SLOT) % blocks) == (line // rows)
    which_slot = (column % SLOT).astype(F32)

    def stacked(m):
        return jnp.concatenate([tok[m, :, b * LANES : (b + 1) * LANES] for b in range(blocks)], axis=0)

    upright = iota((rows, rows), 0) == iota((rows, rows), 1)

    def columns(flat):
        zero = jnp.zeros((), flat.dtype)
        return [
            jnp.sum(jnp.where(upright, flat[k : k + 1], zero), axis=1, keepdims=True)
            for k in range(flat.shape[0])
        ]

    def relative(m):
        found = []
        for named in columns(ids[m]):
            rel = (((named // ZN) - y + YN) % YN) * ZN + (((named % ZN) - z + ZN) % ZN)
            found.append(jnp.concatenate([rel] * blocks, axis=0))
        return found

    def choose(m):
        hit = sum((rel == lane).astype(F32) for rel in relative(m))
        position = jnp.dot(earlier, hit.astype(BF), preferred_element_type=F32)
        code = jnp.where(hit > 0, position, -1.0).astype(BF)
        full = jnp.dot(code, spread, preferred_element_type=F32)
        chosen = jnp.where(fits & (full == which_slot), 1.0, 0.0).astype(BF)
        sel[m] = chosen
        moved = lax.dot_general(
            chosen, stacked(m), (((0,), (0,)), ((), ())), preferred_element_type=F32
        )
        sb[:, m * per : (m + 1) * per, :] = moved.astype(BF).reshape(groups, per, LANES)

    for q in copies[:2]:
        q.wait()
    for m in range(batches):
        choose(m)
    rb[0] = sb[0]

    gain_row = gain[...].astype(F32).reshape(1, chan)
    values = tok[...].reshape(batches * rows, chan).astype(F32)
    scaled = values * gain_row
    high = scaled.astype(BF)
    low = (scaled - high.astype(F32)).astype(BF)
    copies[2].wait()
    across = (((1,), (1,)), ((), ()))
    part = lax.dot_general(high, router[...], across, preferred_element_type=F32)
    part = part + lax.dot_general(low, router[...], across, preferred_element_type=F32)
    squares = jnp.sum(values * values, axis=1, keepdims=True)
    place_of = iota((rows, router.shape[0]), 1)

    def flatten(column):
        return jnp.sum(jnp.where(upright, column, 0.0), axis=0, keepdims=True)

    gx[0] = jnp.zeros(gx.shape[1:], F32)
    for m in range(batches):
        these = slice(m * rows, (m + 1) * rows)
        named = columns(ids[m])
        for k, one in enumerate(named):
            mine = jnp.sum(jnp.where(one == place_of, part[these], 0.0), axis=1, keepdims=True)
            gx[0, m, k : k + 1, :] = flatten(mine)
        gx[0, m, len(named) : len(named) + 1, :] = flatten(squares[these])

    pl.semaphore_wait(barrier, groups - 1 + len(mates))

    def far_first(s):
        return sorted(range(max(s * ZN, 1), (s + 1) * ZN), key=lambda d: -min(d % ZN, ZN - d % ZN))

    def whole(s, src, dst, send, recv):
        some = pl.ds(max(s * ZN, 1), ZN - (s == 0))
        q = remote(src.at[some], dst.at[some], send.at[s], recv.at[s], right)
        sent.append(q)
        return q

    def z_out(s):
        for d in far_first(s):
            remote(sb.at[d], rb.at[d], z_s.at[s], z_r.at[s], ahead(d)).start()
        coming["z", s] = whole(s, sb, rb, z_s, z_r)

    def gx_send():
        for cs, xr in mates:
            there = cs * XN + (XN - xr) % XN
            remote(gx.at[0], gx.at[there], gx_s, gx_r, near(cs, xr)).start()
        rest = pl.ds(1, CN * XN - 1)
        q = remote(gx.at[rest], gx.at[rest], gx_s, gx_r, other)
        sent.append(q)
        coming["g",] = q

    tile = ZN * per
    i_to, i_from = iota((tile, tile), 0), iota((tile, tile), 1)
    to_b, to_d, to_p = i_to // (ZN * SLOT), (i_to // SLOT) % ZN, i_to % SLOT
    apart = (i_from == to_d * per + to_b * SLOT + to_p).astype(BF)
    from_b, from_d, from_p = i_from // (ZN * SLOT), (i_from // SLOT) % ZN, i_from % SLOT
    together = (i_to == from_d * per + from_b * SLOT + from_p).astype(BF)
    chunk = ZN * SLOT
    diagonal = iota((slots, slots), 0) == iota((slots, slots), 1)

    def x_copy(s, i, src, dst, peer):
        launch(("x", s, i), remote(src, dst, x_s.at[s, i], x_r.at[s, i], peer))

    lower, upper = pl.ds(0, slots // 2), pl.ds(slots // 2, slots // 2)

    def arrive(s):
        receive("z", s)
        squares = []
        for n in range(batches):
            raw = rb[s * ZN + n * step : s * ZN + (n + 1) * step].reshape(tile, LANES)
            moved = jnp.dot(apart, raw, preferred_element_type=F32)
            part = jnp.concatenate([moved[b * chunk : (b + 1) * chunk] for b in range(blocks)], axis=1)
            squares.append(jnp.sum(part * part, axis=1, keepdims=True))
            xb[s, 0, 0, n * chunk : (n + 1) * chunk, :] = (part * gain_row).astype(BF)
        own = xb.at[s, 0, 0]
        x_copy(s, 0, own.at[lower], xb.at[s, 0, XN - 1, lower], right)
        x_copy(s, 1, own.at[upper], xb.at[s, 0, 1, upper], left)
        x_copy(s, 2, own.at[upper], xb.at[s, 0, XN - 1, upper], right)
        x_copy(s, 3, own.at[lower], xb.at[s, 0, 1, lower], left)
        x_copy(s, 4, own, xb.at[s, 1, 0], other)
        square = jnp.concatenate(squares, axis=0)
        flat = jnp.sum(jnp.where(diagonal, square, 0.0), axis=0, keepdims=True)
        mt[s, 0] = jnp.broadcast_to(flat, mt.shape[2:])
        for cs, xr in mates:
            there = cs * XN + (XN - xr) % XN
            remote(mt.at[s, 0], mt.at[s, there], m_s.at[s], m_r.at[s], near(cs, xr)).start()
        rest = pl.ds(1, CN * XN - 1)
        q = remote(mt.at[s, rest], mt.at[s, rest], m_s.at[s], m_r.at[s], other)
        sent.append(q)
        coming["m", s] = q

    def relay(s):
        receive("x", s, 0)
        x_copy(s, 5, xb.at[s, 0, XN - 1, lower], xb.at[s, 0, 2, lower], right)
        receive("x", s, 1)
        x_copy(s, 6, xb.at[s, 0, 1, upper], xb.at[s, 0, 2, upper], left)
        receive("x", s, 2)
        x_copy(s, 7, xb.at[s, 0, XN - 1], xb.at[s, 1, XN - 1], other)
        receive("x", s, 3)
        x_copy(s, 8, xb.at[s, 0, 1], xb.at[s, 1, 1], other)

    def hidden(s):
        receive("x", s, 5)
        receive("x", s, 6)
        x_copy(s, 9, xb.at[s, 0, 2], xb.at[s, 1, 2], other)
        acts = jnp.zeros((slots, 2 * hid), F32)
        for xr in range(XN):
            acts = acts + jnp.dot(xb[s, 0, xr], wgu[xr], preferred_element_type=F32)
        receive("m", s)
        total = sum(mt[s, r] for r in range(CN * XN))
        inv = lax.rsqrt(total[0:1] / depth + 1e-06)
        inv = jnp.sum(jnp.where(diagonal, inv, 0.0), axis=1, keepdims=True)
        for i, xr in ((4, 0), (7, XN - 1), (8, 1), (9, 2)):
            receive("x", s, i)
            acts = acts + jnp.dot(xb[s, 1, xr], wgu[XN + xr], preferred_element_type=F32)
        acts = acts * inv
        gate, up = acts[:, :hid], acts[:, hid:]
        hb[s, 0, 0] = (gate / (1.0 + jnp.exp(-gate)) * up).astype(BF)
        for xr in (2, 1, 3):
            there = hb.at[s, 0, XN - xr]
            launch(("h", s, 0, XN - xr), remote(hb.at[s, 0, 0], there, h_s.at[s, xr], h_r.at[s, XN - xr], near(0, xr)))
        launch(("h", s, 1, 0), remote(hb.at[s, 0, 0], hb.at[s, 1, 0], h_s.at[s, 0], h_r.at[s, 0], other))

    def hidden_relay(s):
        for xr in (1, 3, 2):
            receive("h", s, 0, xr)
            there = hb.at[s, 1, xr]
            launch(("h", s, 1, xr), remote(hb.at[s, 0, xr], there, h_s.at[s, XN + xr], h_r.at[s, XN + xr], other))

    def give_back(s):
        done = jnp.zeros((slots, chan), F32)
        for xr in range(XN):
            done = done + jnp.dot(hb[s, 0, xr], wdv[xr], preferred_element_type=F32)
        for xr in (0, 1, 3, 2):
            receive("h", s, 1, xr)
            done = done + jnp.dot(hb[s, 1, xr], wdv[XN + xr], preferred_element_type=F32)
        done = done.astype(BF)
        for n in range(batches):
            part = done[n * chunk : (n + 1) * chunk]
            part = jnp.concatenate([part[:, b * LANES : (b + 1) * LANES] for b in range(blocks)], axis=0)
            moved = jnp.dot(together, part, preferred_element_type=F32).astype(BF)
            ob[s * ZN + n * step : s * ZN + (n + 1) * step] = moved.reshape(step, batches * per, LANES)
        for d in far_first(s):
            remote(ob.at[d], back.at[d], o_s.at[s], o_r.at[s], behind(d)).start()
        if s == 0:
            back[0] = ob[0]
        coming["o", s] = whole(s, ob, back, o_s, o_r)

    def weigh():
        receive("g")
        for m in range(batches):
            picks = ids.shape[1]
            total = sum(gx[r, m] for r in range(CN * XN))
            inv = lax.rsqrt(total[picks : picks + 1] / depth + 1e-06)
            scores = 1.0 / (1.0 + jnp.exp(-(inv * total[0:picks])))
            shares = 2.5 * scores / jnp.sum(scores, axis=0, keepdims=True)
            weight = jnp.zeros((tall, LANES), F32)
            for rel, share in zip(relative(m), columns(shares), strict=True):
                weight = weight + jnp.where(rel == lane, jnp.concatenate([share] * blocks, axis=0), 0.0)
            high = weight.astype(BF)
            low = (weight - high.astype(F32)).astype(BF)
            for i, some in enumerate((high, low)):
                full = jnp.dot(some, spread, preferred_element_type=F32)
                gates[i, m] = full.astype(BF) * sel[m]

    def combine():
        totals = [stacked(m).astype(F32) for m in range(batches)]
        for s in range(YN):
            receive("o", s)
            for m in range(batches):
                part = back[s * ZN : (s + 1) * ZN, m * per : (m + 1) * per, :].reshape(ZN * per, LANES)
                for i in range(2):
                    some = gates[i, m, :, s * ZN * per : (s + 1) * ZN * per]
                    totals[m] = totals[m] + jnp.dot(some, part, preferred_element_type=F32)
        for m, total in enumerate(totals):
            total = total.astype(out.dtype)
            for b in range(blocks):
                out[m, :, b * LANES : (b + 1) * LANES] = total[b * rows : (b + 1) * rows]

    def weights_ready():
        pltpu.make_async_copy(wgu, wgu, wsem.at[0]).wait()
        pltpu.make_async_copy(wdv, wdv, wsem.at[1]).wait()

    for s in range(YN):
        z_out(s)
    gx_send()
    weights_ready()
    arrive(0)
    relay(0)
    arrive(1)
    hidden(0)
    relay(1)
    weigh()
    arrive(2)
    hidden_relay(0)
    hidden(1)
    relay(2)
    give_back(0)
    arrive(3)
    hidden_relay(1)
    hidden(2)
    relay(3)
    give_back(1)
    hidden_relay(2)
    hidden(3)
    give_back(2)
    hidden_relay(3)
    give_back(3)
    combine()

    for q in sent:
        q.wait_send()


def per_device(tokens, norm_gain, router_weight, expert_ids, w_gate, w_up, w_down):
    batches, rows, chan = tokens.shape
    groups = YN * ZN
    per = chan // LANES * SLOT
    hid = w_gate.shape[2]
    stages = YN
    slots = ZN * batches * SLOT
    mates = CN * XN
    tall = chan // LANES * rows
    vmem = pl.BlockSpec(memory_space=pltpu.VMEM)
    hbm = pl.BlockSpec(memory_space=pltpu.HBM)
    dma = pltpu.SemaphoreType.DMA
    blocks = pltpu.VMEM((groups, batches * per, LANES), BF)
    return pl.pallas_call(
        kernel,
        out_shape=jax.ShapeDtypeStruct(tokens.shape, tokens.dtype),
        in_specs=[hbm, vmem] + [hbm] * 5,
        out_specs=vmem,
        scratch_shapes=[
            pltpu.VMEM(tokens.shape, tokens.dtype),
            pltpu.VMEM(router_weight.shape[::-1], router_weight.dtype),
            pltpu.VMEM((batches, expert_ids.shape[2], rows), expert_ids.dtype),
            pltpu.VMEM((mates, chan, 2 * hid), BF),
            pltpu.VMEM((mates, hid, chan), BF),
            pltpu.VMEM((batches, tall, groups * per), BF),
            pltpu.VMEM((2, batches, tall, groups * per), BF),
            pltpu.VMEM((mates, batches, 8, rows), F32),
            blocks,
            blocks,
            pltpu.VMEM((stages, CN, XN, slots, chan), BF),
            pltpu.VMEM((stages, mates, 8, slots), F32),
            pltpu.VMEM((stages, CN, XN, slots, hid), BF),
            blocks,
            blocks,
            dma((5,)),
            dma,
            dma,
            dma((stages,)),
            dma((stages,)),
            dma((stages, 10)),
            dma((stages, 10)),
            dma((stages,)),
            dma((stages,)),
            dma((stages, mates)),
            dma((stages, mates)),
            dma((stages,)),
            dma((stages,)),
        ],
        compiler_params=pltpu.CompilerParams(
            collective_id=0, has_side_effects=True, vmem_limit_bytes=(64 << 20) - (128 << 10)
        ),
        name="routed_experts",
    )(
        tokens,
        norm_gain,
        router_weight.T,
        expert_ids.transpose(0, 2, 1),
        w_gate,
        w_up,
        w_down,
    )


def solution(mesh):
    placed = (
        P(None, "group", ("side", "tensor")),
        P(("side", "tensor")),
        P(("side", "tensor"), None),
        P(None, "group", None),
        P("group", None, ("side", "tensor")),
        P("group", None, ("side", "tensor")),
        P("group", None, ("side", "tensor")),
    )
    return jax.shard_map(
        per_device,
        mesh=mesh,
        in_specs=placed,
        out_specs=P(None, "group", ("side", "tensor")),
        check_vma=False,
    )
```

```python
import jax
import jax.numpy as jnp
from jax import lax
from jax.experimental import pallas as pl
from jax.experimental.pallas import tpu as pltpu
from jax.sharding import PartitionSpec as P

MESH = pl.DeviceIdType.MESH
BF = jnp.bfloat16
F32 = jnp.float32
YN, ZN = 4, 16
XN, CN = 4, 2
SLOT = 4
LANES = 128


def iota(shape, dim):
    return lax.broadcasted_iota(jnp.int32, shape, dim)


def remote(src, dst, send, recv, peer):
    return pltpu.make_async_remote_copy(
        src_ref=src,
        dst_ref=dst,
        send_sem=send,
        recv_sem=recv,
        device_id=peer,
        device_id_type=MESH,
    )


def kernel(
    tok_in, gain, router_in, ids_in, wg, wu, wd, out,
    tok, router, ids, wgu, wdv, sel, gates, gx, sb, rb, xb, mt, hb, ob, back,
    wsem, gx_s, gx_r, z_s, z_r, x_s, x_r, m_s, m_r, h_s, h_r, o_s, o_r,
):
    batches, rows, chan = tok.shape
    groups = YN * ZN
    blocks = chan // LANES
    per = blocks * SLOT
    hid = wg.shape[2]
    depth = CN * XN * chan
    slots = ZN * batches * SLOT
    step = ZN // batches

    g, t, c = (lax.axis_index(a) for a in ("group", "tensor", "side"))
    y, z = lax.div(g, ZN), lax.rem(g, ZN)

    y_at = [lax.rem(y + i, YN) * ZN for i in range(YN)]
    z_at = [lax.rem(z + i, ZN) for i in range(ZN)]

    def ahead(d):
        return {"group": y_at[d // ZN] + z_at[d % ZN]}

    def behind(d):
        return {"group": y_at[-(d // ZN) % YN] + z_at[-(d % ZN) % ZN]}

    def near(cs, xr):
        return {"side": lax.rem(c + cs, CN), "tensor": lax.rem(t + xr, XN)}

    right, left, other = near(0, 1), near(0, XN - 1), near(1, 0)
    mates = [(cs, xr) for cs in range(CN) for xr in range(XN) if cs + xr]

    sent, coming = [], {}

    def launch(key, q):
        q.start()
        sent.append(q)
        coming[key] = q

    def receive(*key):
        coming.pop(key).wait_recv()

    barrier = pltpu.get_barrier_semaphore()

    for d in sorted(range(1, groups), key=lambda d: -min(d % ZN, ZN - d % ZN)):
        pl.semaphore_signal(barrier, inc=1, device_id=ahead(d), device_id_type=MESH)
    for cs, xr in mates:
        pl.semaphore_signal(barrier, inc=1, device_id=near(cs, xr), device_id_type=MESH)

    copies = [
        pltpu.make_async_copy(src, dst, wsem.at[2 + i])
        for i, (src, dst) in enumerate(((ids_in, ids), (tok_in, tok), (router_in, router)))
    ]
    for q in copies:
        q.start()

    for cs in range(CN):
        for xr in range(XN):
            rel = cs * XN + xr
            home = lax.rem(c + cs, CN) * XN + lax.rem(t + xr, XN)
            deep = pl.ds(pl.multiple_of(home * chan, chan), chan)
            pltpu.make_async_copy(wg.at[0, deep, :], wgu.at[rel, :, pl.ds(0, hid)], wsem.at[0]).start()
            pltpu.make_async_copy(wu.at[0, deep, :], wgu.at[rel, :, pl.ds(hid, hid)], wsem.at[0]).start()
            thin = pl.ds(pl.multiple_of(home * hid, hid), hid)
            pltpu.make_async_copy(wd.at[0, thin, :], wdv.at[rel], wsem.at[1]).start()

    tall = blocks * rows
    lane, sub = iota((tall, LANES), 1), iota((tall, LANES), 0)
    earlier = (((sub // rows) == (lane // rows)) & (lane < sub)).astype(BF)
    wide = groups * per
    spread = (iota((LANES, wide), 1) // per == iota((LANES, wide), 0)).astype(BF)
    column, line = iota((tall, wide), 1), iota((tall, wide), 0)
    fits = ((column // SLOT) % blocks) == (line // rows)
    which_slot = (column % SLOT).astype(F32)

    def stacked(m):
        return jnp.concatenate([tok[m, :, b * LANES : (b + 1) * LANES] for b in range(blocks)], axis=0)

    upright = iota((rows, rows), 0) == iota((rows, rows), 1)

    def columns(flat):
        zero = jnp.zeros((), flat.dtype)
        return [
            jnp.sum(jnp.where(upright, flat[k : k + 1], zero), axis=1, keepdims=True)
            for k in range(flat.shape[0])
        ]

    def relative(m):
        found = []
        for named in columns(ids[m]):
            rel = (((named // ZN) - y + YN) % YN) * ZN + (((named % ZN) - z + ZN) % ZN)
            found.append(jnp.concatenate([rel] * blocks, axis=0))
        return found

    def choose(m):
        hit = sum((rel == lane).astype(F32) for rel in relative(m))
        position = jnp.dot(earlier, hit.astype(BF), preferred_element_type=F32)
        code = jnp.where(hit > 0, position, -1.0).astype(BF)
        full = jnp.dot(code, spread, preferred_element_type=F32)
        chosen = jnp.where(fits & (full == which_slot), 1.0, 0.0).astype(BF)
        sel[m] = chosen
        moved = lax.dot_general(
            chosen, stacked(m), (((0,), (0,)), ((), ())), preferred_element_type=F32
        )
        sb[:, m * per : (m + 1) * per, :] = moved.astype(BF).reshape(groups, per, LANES)

    for q in copies[:2]:
        q.wait()
    for m in range(batches):
        choose(m)
    rb[0] = sb[0]

    gain_row = gain[...].astype(F32).reshape(1, chan)
    values = tok[...].reshape(batches * rows, chan).astype(F32)
    scaled = values * gain_row
    high = scaled.astype(BF)
    low = (scaled - high.astype(F32)).astype(BF)
    copies[2].wait()
    across = (((1,), (1,)), ((), ()))
    part = lax.dot_general(high, router[...], across, preferred_element_type=F32)
    part = part + lax.dot_general(low, router[...], across, preferred_element_type=F32)
    squares = jnp.sum(values * values, axis=1, keepdims=True)
    place_of = iota((rows, router.shape[0]), 1)

    def flatten(column):
        return jnp.sum(jnp.where(upright, column, 0.0), axis=0, keepdims=True)

    gx[0] = jnp.zeros(gx.shape[1:], F32)
    for m in range(batches):
        these = slice(m * rows, (m + 1) * rows)
        named = columns(ids[m])
        for k, one in enumerate(named):
            mine = jnp.sum(jnp.where(one == place_of, part[these], 0.0), axis=1, keepdims=True)
            gx[0, m, k : k + 1, :] = flatten(mine)
        gx[0, m, len(named) : len(named) + 1, :] = flatten(squares[these])

    tile = ZN * per
    i_to, i_from = iota((tile, tile), 0), iota((tile, tile), 1)
    to_b, to_d, to_p = i_to // (ZN * SLOT), (i_to // SLOT) % ZN, i_to % SLOT
    apart = (i_from == to_d * per + to_b * SLOT + to_p).astype(BF)
    from_b, from_d, from_p = i_from // (ZN * SLOT), (i_from // SLOT) % ZN, i_from % SLOT
    together = (i_to == from_d * per + from_b * SLOT + from_p).astype(BF)
    chunk = ZN * SLOT
    diagonal = iota((slots, slots), 0) == iota((slots, slots), 1)

    pl.semaphore_wait(barrier, groups - 1 + len(mates))

    def far_first(s):
        return sorted(range(max(s * ZN, 1), (s + 1) * ZN), key=lambda d: -min(d % ZN, ZN - d % ZN))

    def whole(s, src, dst, send, recv):
        some = pl.ds(max(s * ZN, 1), ZN - (s == 0))
        q = remote(src.at[some], dst.at[some], send.at[s], recv.at[s], right)
        sent.append(q)
        return q

    def z_out(s):
        for d in far_first(s):
            remote(sb.at[d], rb.at[d], z_s.at[s], z_r.at[s], ahead(d)).start()
        coming["z", s] = whole(s, sb, rb, z_s, z_r)

    def gx_send():
        for cs, xr in mates:
            there = cs * XN + (XN - xr) % XN
            remote(gx.at[0], gx.at[there], gx_s, gx_r, near(cs, xr)).start()
        rest = pl.ds(1, CN * XN - 1)
        q = remote(gx.at[rest], gx.at[rest], gx_s, gx_r, other)
        sent.append(q)
        coming["g",] = q

    def x_copy(s, i, src, dst, peer):
        launch(("x", s, i), remote(src, dst, x_s.at[s, i], x_r.at[s, i], peer))

    lower, upper = pl.ds(0, slots // 2), pl.ds(slots // 2, slots // 2)

    def arrive(s):
        receive("z", s)
        squares = []
        for n in range(batches):
            raw = rb[s * ZN + n * step : s * ZN + (n + 1) * step].reshape(tile, LANES)
            moved = jnp.dot(apart, raw, preferred_element_type=F32)
            part = jnp.concatenate([moved[b * chunk : (b + 1) * chunk] for b in range(blocks)], axis=1)
            squares.append(jnp.sum(part * part, axis=1, keepdims=True))
            xb[s, 0, 0, n * chunk : (n + 1) * chunk, :] = (part * gain_row).astype(BF)
        own = xb.at[s, 0, 0]
        x_copy(s, 0, own.at[lower], xb.at[s, 0, XN - 1, lower], right)
        x_copy(s, 1, own.at[upper], xb.at[s, 0, 1, upper], left)
        x_copy(s, 2, own.at[upper], xb.at[s, 0, XN - 1, upper], right)
        x_copy(s, 3, own.at[lower], xb.at[s, 0, 1, lower], left)
        x_copy(s, 4, own, xb.at[s, 1, 0], other)
        square = jnp.concatenate(squares, axis=0)
        flat = jnp.sum(jnp.where(diagonal, square, 0.0), axis=0, keepdims=True)
        mt[s, 0] = flat
        for cs, xr in mates:
            there = cs * XN + (XN - xr) % XN
            remote(mt.at[s, 0], mt.at[s, there], m_s.at[s], m_r.at[s], near(cs, xr)).start()
        rest = pl.ds(1, CN * XN - 1)
        q = remote(mt.at[s, rest], mt.at[s, rest], m_s.at[s], m_r.at[s], other)
        sent.append(q)
        coming["m", s] = q

    def relay(s):
        receive("x", s, 0)
        x_copy(s, 5, xb.at[s, 0, XN - 1, lower], xb.at[s, 0, 2, lower], right)
        receive("x", s, 1)
        x_copy(s, 6, xb.at[s, 0, 1, upper], xb.at[s, 0, 2, upper], left)
        receive("x", s, 2)
        x_copy(s, 7, xb.at[s, 0, XN - 1], xb.at[s, 1, XN - 1], other)
        receive("x", s, 3)
        x_copy(s, 8, xb.at[s, 0, 1], xb.at[s, 1, 1], other)

    def hidden(s):
        receive("x", s, 5)
        receive("x", s, 6)
        x_copy(s, 9, xb.at[s, 0, 2], xb.at[s, 1, 2], other)
        acts = jnp.zeros((slots, 2 * hid), F32)
        for xr in range(XN):
            acts = acts + jnp.dot(xb[s, 0, xr], wgu[xr], preferred_element_type=F32)
        receive("m", s)
        total = sum(mt[s, r] for r in range(CN * XN))
        inv = lax.rsqrt(total / depth + 1e-06)
        inv = jnp.sum(jnp.where(diagonal, inv, 0.0), axis=1, keepdims=True)
        for i, xr in ((4, 0), (7, XN - 1), (8, 1), (9, 2)):
            receive("x", s, i)
            acts = acts + jnp.dot(xb[s, 1, xr], wgu[XN + xr], preferred_element_type=F32)
        acts = acts * inv
        gate, up = acts[:, :hid], acts[:, hid:]
        hb[s, 0, 0] = (gate / (1.0 + jnp.exp(-gate)) * up).astype(BF)
        for xr in (2, 1, 3):
            there = hb.at[s, 0, XN - xr]
            launch(("h", s, 0, XN - xr), remote(hb.at[s, 0, 0], there, h_s.at[s, xr], h_r.at[s, XN - xr], near(0, xr)))
        launch(("h", s, 1, 0), remote(hb.at[s, 0, 0], hb.at[s, 1, 0], h_s.at[s, 0], h_r.at[s, 0], other))

    def hidden_relay(s):
        for xr in (1, 3, 2):
            receive("h", s, 0, xr)
            there = hb.at[s, 1, xr]
            launch(("h", s, 1, xr), remote(hb.at[s, 0, xr], there, h_s.at[s, XN + xr], h_r.at[s, XN + xr], other))

    def give_back(s):
        done = jnp.zeros((slots, chan), F32)
        for xr in range(XN):
            done = done + jnp.dot(hb[s, 0, xr], wdv[xr], preferred_element_type=F32)
        for xr in (0, 1, 3, 2):
            receive("h", s, 1, xr)
            done = done + jnp.dot(hb[s, 1, xr], wdv[XN + xr], preferred_element_type=F32)
        done = done.astype(BF)
        for n in range(batches):
            part = done[n * chunk : (n + 1) * chunk]
            part = jnp.concatenate([part[:, b * LANES : (b + 1) * LANES] for b in range(blocks)], axis=0)
            moved = jnp.dot(together, part, preferred_element_type=F32).astype(BF)
            ob[s * ZN + n * step : s * ZN + (n + 1) * step] = moved.reshape(step, batches * per, LANES)
        for d in far_first(s):
            remote(ob.at[d], back.at[d], o_s.at[s], o_r.at[s], behind(d)).start()
        if s == 0:
            back[0] = ob[0]
        coming["o", s] = whole(s, ob, back, o_s, o_r)

    def weigh():
        receive("g")
        for m in range(batches):
            picks = ids.shape[1]
            total = sum(gx[r, m] for r in range(CN * XN))
            inv = lax.rsqrt(total[picks : picks + 1] / depth + 1e-06)
            scores = 1.0 / (1.0 + jnp.exp(-(inv * total[0:picks])))
            shares = 2.5 * scores / jnp.sum(scores, axis=0, keepdims=True)
            weight = jnp.zeros((tall, LANES), F32)
            for rel, share in zip(relative(m), columns(shares), strict=True):
                weight = weight + jnp.where(rel == lane, jnp.concatenate([share] * blocks, axis=0), 0.0)
            high = weight.astype(BF)
            low = (weight - high.astype(F32)).astype(BF)
            for i, some in enumerate((high, low)):
                full = jnp.dot(some, spread, preferred_element_type=F32)
                gates[i, m] = full.astype(BF) * sel[m]

    def combine():
        totals = [stacked(m).astype(F32) for m in range(batches)]
        for s in range(YN):
            receive("o", s)
            for m in range(batches):
                part = back[s * ZN : (s + 1) * ZN, m * per : (m + 1) * per, :].reshape(ZN * per, LANES)
                for i in range(2):
                    some = gates[i, m, :, s * ZN * per : (s + 1) * ZN * per]
                    totals[m] = totals[m] + jnp.dot(some, part, preferred_element_type=F32)
        for m, total in enumerate(totals):
            total = total.astype(out.dtype)
            for b in range(blocks):
                out[m, :, b * LANES : (b + 1) * LANES] = total[b * rows : (b + 1) * rows]

    def weights_ready():
        pltpu.make_async_copy(wgu, wgu, wsem.at[0]).wait()
        pltpu.make_async_copy(wdv, wdv, wsem.at[1]).wait()

    for s in range(YN):
        z_out(s)
    gx_send()
    weights_ready()
    arrive(0)
    relay(0)
    arrive(1)
    hidden(0)
    relay(1)
    weigh()
    arrive(2)
    hidden_relay(0)
    hidden(1)
    relay(2)
    give_back(0)
    arrive(3)
    hidden_relay(1)
    hidden(2)
    relay(3)
    give_back(1)
    hidden_relay(2)
    hidden(3)
    give_back(2)
    hidden_relay(3)
    give_back(3)
    combine()

    for q in sent:
        q.wait_send()


def per_device(tokens, norm_gain, router_weight, expert_ids, w_gate, w_up, w_down):
    batches, rows, chan = tokens.shape
    groups = YN * ZN
    per = chan // LANES * SLOT
    hid = w_gate.shape[2]
    stages = YN
    slots = ZN * batches * SLOT
    mates = CN * XN
    tall = chan // LANES * rows
    vmem = pl.BlockSpec(memory_space=pltpu.VMEM)
    hbm = pl.BlockSpec(memory_space=pltpu.HBM)
    dma = pltpu.SemaphoreType.DMA
    blocks = pltpu.VMEM((groups, batches * per, LANES), BF)
    return pl.pallas_call(
        kernel,
        out_shape=jax.ShapeDtypeStruct(tokens.shape, tokens.dtype),
        in_specs=[hbm, vmem] + [hbm] * 5,
        out_specs=vmem,
        scratch_shapes=[
            pltpu.VMEM(tokens.shape, tokens.dtype),
            pltpu.VMEM(router_weight.shape[::-1], router_weight.dtype),
            pltpu.VMEM((batches, expert_ids.shape[2], rows), expert_ids.dtype),
            pltpu.VMEM((mates, chan, 2 * hid), BF),
            pltpu.VMEM((mates, hid, chan), BF),
            pltpu.VMEM((batches, tall, groups * per), BF),
            pltpu.VMEM((2, batches, tall, groups * per), BF),
            pltpu.VMEM((mates, batches, 8, rows), F32),
            blocks,
            blocks,
            pltpu.VMEM((stages, CN, XN, slots, chan), BF),
            pltpu.VMEM((stages, mates, 1, slots), F32),
            pltpu.VMEM((stages, CN, XN, slots, hid), BF),
            blocks,
            blocks,
            dma((5,)),
            dma,
            dma,
            dma((stages,)),
            dma((stages,)),
            dma((stages, 10)),
            dma((stages, 10)),
            dma((stages,)),
            dma((stages,)),
            dma((stages, mates)),
            dma((stages, mates)),
            dma((stages,)),
            dma((stages,)),
        ],
        compiler_params=pltpu.CompilerParams(
            collective_id=0, has_side_effects=True, vmem_limit_bytes=(64 << 20) - (128 << 10)
        ),
        name="routed_experts",
    )(
        tokens,
        norm_gain,
        router_weight.T,
        expert_ids.transpose(0, 2, 1),
        w_gate,
        w_up,
        w_down,
    )


def solution(mesh):
    placed = (
        P(None, "group", ("side", "tensor")),
        P(("side", "tensor")),
        P(("side", "tensor"), None),
        P(None, "group", None),
        P("group", None, ("side", "tensor")),
        P("group", None, ("side", "tensor")),
        P("group", None, ("side", "tensor")),
    )
    return jax.shard_map(
        per_device,
        mesh=mesh,
        in_specs=placed,
        out_specs=P(None, "group", ("side", "tensor")),
        check_vma=False,
    )
```
